32 devices in a mesh: seq: 8 (over z, y), ch: 4 (over x, core).
Axes of the slice: x: 2, y: 2, z: 4, core: 2. Of those that a mesh axis runs over, the one named last changes fastest.
Arguments:
- frames_in: bfloat16 [16384, 1024], P('seq'), may hold values from -6 to 6
- w_in: bfloat16 [1024, 3, 1024], P(None, None, 'ch'), may hold values from -0.1875 to 0.1875
- filters: bfloat16 [16384, 1024], P('seq', 'ch'), may hold values from -1.5 to 1.5
- skip_gain: float32 [1024], P('ch'), may hold values from -1 to 1
- w_out: bfloat16 [1024, 1024], P('ch'), may hold values from -0.1875 to 0.1875
Outputs:
- mixed: bfloat16 [16384, 1024], P('seq', 'ch')
The draws below stay inside these ranges and needn't reach their ends.
All inputs are finite; a program needn't handle non-finite values.
Results may differ from the reference program's by a relative error of at most 0.01.
Values may be sent and summed in bfloat16 or wider, within the bound.
No kernel may reach another device: no remote copies, remote signals or barrier semaphores. Data moves between devices by JAX's collectives and lax.ppermute only.
A program may use at most 128 MiB of HBM per device.

```python
import math
import jax
import jax.numpy as jnp
from jax import lax

D = 1024
FRAMES = 16384


def draw_filters(key, part):
    key_fast = jax.random.fold_in(key, 11)
    key_slow = jax.random.fold_in(key, 12)
    key_coin = jax.random.fold_in(key, 13)
    key_rough = jax.random.fold_in(key, 14)
    fast_decay = jnp.exp(jax.random.uniform(key_fast, (D,), jnp.float32, math.log(10.0), math.log(40.0)))
    slow_decay = jnp.exp(jax.random.uniform(key_slow, (D,), jnp.float32, jnp.log(0.5 * FRAMES), jnp.log(8.0 * FRAMES)))
    long_share = 0.5
    keeps_long = jax.random.uniform(key_coin, (D,), jnp.float32) < long_share
    decay_len = jnp.where(keeps_long, slow_decay, fast_decay)
    amplitude = jax.lax.rsqrt(0.5 * decay_len * (1.0 - jnp.exp(-2.0 * FRAMES / decay_len)))
    position = jnp.arange(FRAMES, dtype=jnp.float32)[:, None]
    roughness = jax.random.truncated_normal(key_rough, -3.0, 3.0, (FRAMES, D), jnp.float32)
    values = amplitude[None, :] * jnp.exp(-position / decay_len[None, :]) * roughness
    return values.astype(jnp.bfloat16)


def levels(own_key, extent, shards, smallest, top_value):
    def one(dim, parts):
        heights = jax.random.uniform(jax.random.fold_in(jax.random.fold_in(own_key, 6), dim), (parts,), jnp.float32, smallest / len(shards), top_value / len(shards))
        return jnp.repeat(jnp.exp(heights), extent[dim] // parts).reshape((-1,) + (1,) * (len(extent) - dim - 1))

    factor_of = one(*shards[0])
    for cut in shards[1:]:
        factor_of = factor_of * one(*cut)
    return factor_of


def gaussian(rng, dims, spread, bound, shards=(), kind=jnp.bfloat16):
    values = jax.random.normal(rng, dims, jnp.float32) * spread
    if len(shards) > 0:
        values = levels(rng, dims, shards, -0.22, 0.18) * values
    return jnp.clip(values, min=-bound, max=bound).astype(kind)


def setup_inputs(seed: int = 0) -> dict:
    key_list = jax.random.split(jax.random.key(seed), 6)
    frames_in = gaussian(key_list[0], (FRAMES, D), 1.0, 6.0, ((0, 8),))
    w_in = gaussian(key_list[1], (D, 3, D), D ** -0.5, 0.1875, ((2, 4),))
    filters = draw_filters(jax.random.fold_in(key_list[5], 71), 0)
    skip_gain = jnp.clip(jax.random.uniform(key_list[3], (D,), jnp.float32, -1.0, 1.0) * levels(key_list[3], (D,), ((0, 4),), -0.4, 0.0), -1.0, 1.0)
    w_out = gaussian(key_list[4], (D, D), D ** -0.5, 0.1875, ((0, 4),))
    return dict(frames_in=frames_in, w_in=w_in, filters=filters, skip_gain=skip_gain, w_out=w_out)


def convolve_block(pair):
    sig_block, filt_block = pair
    total_len = 2 * FRAMES
    spectrum = jnp.fft.rfft(sig_block, n=total_len, axis=1) * jnp.fft.rfft(filt_block, n=total_len, axis=1)
    return jnp.fft.irfft(spectrum, n=total_len, axis=1)[:, :FRAMES]


def reference(frames_in, w_in, filters, skip_gain, w_out):
    projected = jnp.dot(frames_in.astype(jnp.float32), w_in.reshape(D, 3 * D).astype(jnp.float32),
                        precision=lax.Precision.HIGHEST, preferred_element_type=jnp.float32)
    projected = projected.astype(jnp.bfloat16).reshape(FRAMES, 3, D)
    query_gate = projected[:, 0, :].astype(jnp.float32)
    signal = (projected[:, 1, :].astype(jnp.float32) * projected[:, 2, :].astype(jnp.float32)).astype(jnp.bfloat16)
    sig_blocks = signal.astype(jnp.float32).T.reshape(8, D // 8, FRAMES)
    filt_blocks = filters.astype(jnp.float32).T.reshape(8, D // 8, FRAMES)
    convolved = lax.map(convolve_block, (sig_blocks, filt_blocks))
    convolved = convolved.reshape(D, FRAMES).T.astype(jnp.bfloat16)
    gated_out = (query_gate * (convolved.astype(jnp.float32) + skip_gain[None, :] * signal.astype(jnp.float32))).astype(jnp.bfloat16)
    mixed = jnp.dot(gated_out.astype(jnp.float32), w_out.astype(jnp.float32),
                    precision=lax.Precision.HIGHEST, preferred_element_type=jnp.float32)
    return mixed.astype(jnp.bfloat16)
```

```python
import functools
import math

import jax
import jax.numpy as jnp
import numpy as np
from jax import lax
from jax.experimental import pallas as pl
from jax.experimental.pallas import tpu as pltpu
from jax.sharding import PartitionSpec as P

LANES = 128
CHUNKS = 4
BF16 = jnp.bfloat16
F32 = jnp.float32


def dot(left, right):
    return jnp.dot(left, right, preferred_element_type=F32)


def cost(flops, data):
    return pl.CostEstimate(flops=int(flops), bytes_accessed=int(data), transcendentals=0)


def params(mib):
    return pltpu.CompilerParams(vmem_limit_bytes=mib * 1024 * 1024)


def tables(rows):
    total = rows * LANES
    r = np.arange(rows, dtype=np.float64)
    l = np.arange(LANES, dtype=np.float64)
    first = 2 * np.pi * np.outer(r + 0.25, r) / rows
    twist = 2 * np.pi * np.outer(r + 0.25, l) / total
    second = 2 * np.pi * np.outer(l, l) / LANES
    a_fwd = np.concatenate([np.cos(first), -np.sin(first)], 0)
    a_inv = np.concatenate([np.cos(first).T, -np.sin(first).T], 1) / rows
    c2, s2 = np.cos(second), np.sin(second)
    b_fwd = np.block([[c2, -s2], [s2, c2]])
    b_inv = np.block([[c2, s2], [-s2, c2]]) / LANES
    as_bf = lambda v: jnp.asarray(v.astype(np.float32)).astype(BF16)
    as_f = lambda v: jnp.asarray(v.astype(np.float32))
    return (as_bf(a_fwd), as_bf(b_fwd), as_bf(b_inv), as_bf(a_inv), as_f(np.cos(twist)), as_f(np.sin(twist)))


def seq_peer(step):
    return lax.bitwise_xor(lax.axis_index("seq"), jnp.int32(step))


def filter_kernel(seq, cpc, f_ref, *rest):
    outs, (turned,) = rest[:seq], rest[seq:]
    frames, chans = f_ref.shape
    rows = frames // LANES
    group = seq * cpc
    for r in range(rows):
        turned[pl.ds(r, chans, stride=rows), :] = f_ref[pl.ds(r * LANES, LANES), :].astype(F32).T
    for d in range(seq):
        peer = seq_peer(d)
        for k in range(chans // group):
            start = pl.multiple_of((k * group + peer * cpc) * rows, 8)
            part = turned[pl.ds(start, cpc * rows), :].reshape(cpc, rows, LANES)
            outs[d][pl.ds(k * cpc, cpc)] = part.astype(BF16)


def prepare_filters(filters, seq, cpc):
    frames, chans = filters.shape
    rows = frames // LANES
    return pl.pallas_call(
        functools.partial(filter_kernel, seq, cpc),
        out_shape=[jax.ShapeDtypeStruct((chans // seq, rows, LANES), BF16)] * seq,
        scratch_shapes=[pltpu.VMEM((chans * rows, LANES), F32)],
        compiler_params=params(24),
        cost_estimate=cost(0, 8 * frames * chans),
        name="filter_blocks",
    )(filters)


def project_kernel(seq, cpc, x_ref, w_ref, gate_ref, sig_ref, *rest):
    outs, (turned,) = rest[:-1], rest[-1:]
    tile = x_ref.shape[0]
    chans = gate_ref.shape[1]
    step = pl.program_id(0)
    rows_here = tile // LANES
    rows = rows_here * pl.num_programs(0)
    x = x_ref[...]
    gate = dot(x, w_ref[0]).astype(BF16).astype(F32)
    key = dot(x, w_ref[1]).astype(BF16).astype(F32)
    value = dot(x, w_ref[2]).astype(BF16).astype(F32)
    signal = key * value
    for r in range(rows_here):
        here = slice(r * LANES, (r + 1) * LANES)
        gate_ref[r] = gate[here].T.astype(BF16)
        flipped = signal[here].T
        sig_ref[r] = flipped.astype(BF16)
        turned[pl.ds(step * rows_here + r, chans, stride=16), :] = flipped

    @pl.when(step == pl.num_programs(0) - 1)
    def _():
        group = seq * cpc
        for d in range(seq):
            peer = seq_peer(d)
            for k in range(chans // group):
                start = pl.multiple_of((k * group + peer * cpc) * 16, 8)
                part = turned[pl.ds(start, cpc * 16), :].reshape(cpc, 16, LANES)
                outs[d * (chans // group) + k][...] = part.astype(BF16)


def project(frames_in, w_in, seq, cpc):
    frames, width = frames_in.shape
    chans = w_in.shape[2]
    rows = frames // LANES
    tile = 512
    blocks = seq * (chans // (seq * cpc))
    by_row = pl.BlockSpec((tile // LANES, chans, LANES), lambda i: (i, 0, 0))
    whole = lambda *shape: pl.BlockSpec(shape, lambda i: (0,) * len(shape))
    return pl.pallas_call(
        functools.partial(project_kernel, seq, cpc),
        grid=(frames // tile,),
        in_specs=[pl.BlockSpec((tile, width), lambda i: (i, 0)), whole(3, width, chans)],
        out_specs=[by_row, by_row] + [whole(cpc, rows, LANES)] * blocks,
        out_shape=[jax.ShapeDtypeStruct((rows, chans, LANES), BF16)] * 2
        + [jax.ShapeDtypeStruct((cpc, rows, LANES), BF16)] * blocks,
        scratch_shapes=[pltpu.VMEM((chans * rows, LANES), F32)],
        compiler_params=params(40),
        cost_estimate=cost(6 * frames * width * chans, 16 * 1024 * 1024),
        name="project",
    )(frames_in, w_in)


def conv_kernel(seq, cpc, rows, *refs):
    s_refs, f_refs = refs[:seq], refs[seq : 2 * seq]
    a_fwd, b_fwd, b_inv, a_inv, tc_ref, ts_ref = refs[2 * seq : 2 * seq + 6]
    y_refs = refs[2 * seq + 6 : 3 * seq + 6]
    grid_sf, grid_y = refs[3 * seq + 6 :]
    full = rows * seq
    for d in range(seq):
        place = pl.ds(pl.multiple_of(seq_peer(d) * rows, 16), rows)
        grid_sf[:, place, :LANES] = s_refs[d][...]
        grid_sf[:, place, LANES:] = f_refs[d][...]
    for c in range(cpc):
        tc, ts = tc_ref[...], ts_ref[...]
        outer = dot(a_fwd[...], grid_sf[c])
        parts = []
        for side in (slice(0, LANES), slice(LANES, 2 * LANES)):
            re, im = outer[:full, side], outer[full:, side]
            parts.append(
                jnp.concatenate([re * tc + im * ts, im * tc - re * ts], 1).astype(BF16)
            )
        spec_s, spec_f = dot(parts[0], b_fwd[...]), dot(parts[1], b_fwd[...])
        sr, si = spec_s[:, :LANES], spec_s[:, LANES:]
        fr, fi = spec_f[:, :LANES], spec_f[:, LANES:]
        prod = jnp.concatenate([sr * fr - si * fi, sr * fi + si * fr], 1).astype(BF16)
        inner = dot(prod, b_inv[...])
        re, im = inner[:, :LANES], inner[:, LANES:]
        back = jnp.concatenate([re * tc - im * ts, im * tc + re * ts], 0).astype(BF16)
        grid_y[c] = dot(a_inv[...], back).astype(BF16)
    for d in range(seq):
        place = pl.ds(pl.multiple_of(seq_peer(d) * rows, 16), rows)
        y_refs[d][...] = grid_y[:, place, :]


def convolve(sig_blocks, filt_blocks, consts, chunk):
    seq = len(sig_blocks)
    cpc, rows, _ = sig_blocks[0].shape
    full = rows * seq
    block = lambda k: pl.BlockSpec((cpc, rows, LANES), lambda i: (k, 0, 0))
    whole = lambda v: pl.BlockSpec(v.shape, lambda i: (0,) * v.ndim)
    return pl.pallas_call(
        functools.partial(conv_kernel, seq, cpc, rows),
        grid=(1,),
        in_specs=[block(0)] * seq + [block(chunk)] * seq + [whole(v) for v in consts],
        out_specs=[block(0)] * seq,
        out_shape=[jax.ShapeDtypeStruct((cpc, rows, LANES), BF16)] * seq,
        scratch_shapes=[
            pltpu.VMEM((cpc, full, 2 * LANES), BF16),
            pltpu.VMEM((cpc, full, LANES), BF16),
        ],
        compiler_params=params(40),
        cost_estimate=cost(cpc * full * LANES * LANES * 64, cpc * full * LANES * 6),
        name="convolve",
    )(*sig_blocks, *filt_blocks, *consts)


def gate_kernel(seq, cpc, *refs):
    y_refs = refs[:seq]
    gate_ref, sig_ref, skip_ref, out_ref, grid_y = refs[seq:]
    rows, group, _ = out_ref.shape
    for d in range(seq):
        start = pl.multiple_of(seq_peer(d) * (cpc * rows), 8)
        grid_y[pl.ds(start, cpc * rows), :] = (
            y_refs[d][...].astype(F32).reshape(cpc * rows, LANES)
        )
    skip = skip_ref[...]
    for r in range(rows):
        y = grid_y[pl.ds(r, group, stride=rows), :]
        out_ref[r] = (gate_ref[r].astype(F32) * (y + skip * sig_ref[r].astype(F32))).astype(BF16)


def apply_gate(y_blocks, gate, signal, skip, chunk):
    seq = len(y_blocks)
    cpc, rows, _ = y_blocks[0].shape
    group = seq * cpc
    block = pl.BlockSpec((cpc, rows, LANES), lambda i: (0, 0, 0))
    part = pl.BlockSpec((rows, group, LANES), lambda i: (0, chunk, 0))
    return pl.pallas_call(
        functools.partial(gate_kernel, seq, cpc),
        grid=(1,),
        in_specs=[block] * seq + [part, part, pl.BlockSpec((group, 1), lambda i: (chunk, 0))],
        out_specs=pl.BlockSpec((rows, group, LANES), lambda i: (0, 0, 0)),
        out_shape=jax.ShapeDtypeStruct((rows, group, LANES), BF16),
        scratch_shapes=[pltpu.VMEM((group * rows, LANES), F32)],
        compiler_params=params(24),
        cost_estimate=cost(0, 10 * rows * group * LANES),
        name="apply_gate",
    )(*y_blocks, gate, signal, skip)


def out_weights_kernel(ways, w_ref, *outs):
    depth = w_ref.shape[1] // ways
    for d in range(ways):
        peer = lax.bitwise_xor(lax.axis_index("ch"), jnp.int32(d))
        cols = pl.ds(pl.multiple_of(peer * depth, LANES), depth)
        outs[d][...] = w_ref[:, cols].astype(F32).T.astype(BF16)


def out_weights(w_out, ways):
    chans, width = w_out.shape
    return pl.pallas_call(
        functools.partial(out_weights_kernel, ways),
        out_shape=[jax.ShapeDtypeStruct((width // ways, chans), BF16)] * ways,
        compiler_params=params(24),
        cost_estimate=cost(0, 4 * chans * width),
        name="out_weights",
    )(w_out)


def mix_kernel(ways, chunks, *refs):
    w_refs, g_refs, out_ref = refs[:ways], refs[ways:-1], refs[-1]
    rows = g_refs[0].shape[0]
    for r in range(0, rows, 2):
        total = None
        for d in range(ways):
            pieces = g_refs[d * chunks : (d + 1) * chunks]
            left = jnp.concatenate([p[r] for p in pieces], 0)
            right = jnp.concatenate([p[r + 1] for p in pieces], 0)
            term = dot(w_refs[d][...], jnp.concatenate([left, right], 1))
            total = term if total is None else total + term
        out_ref[pl.ds(r * LANES, 2 * LANES), :] = total.T.astype(BF16)


def mix(weights, gated):
    ways, chunks = len(weights), len(gated[0])
    rows, group, _ = gated[0][0].shape
    depth, chans = weights[0].shape
    step = 4
    return pl.pallas_call(
        functools.partial(mix_kernel, ways, chunks),
        grid=(rows // step,),
        in_specs=[pl.BlockSpec((depth, chans), lambda i: (0, 0))] * ways
        + [pl.BlockSpec((step, group, LANES), lambda i: (i, 0, 0))] * (ways * chunks),
        out_specs=pl.BlockSpec((step * LANES, depth), lambda i: (i, 0)),
        out_shape=jax.ShapeDtypeStruct((rows * LANES, depth), BF16),
        compiler_params=params(40),
        cost_estimate=cost(2 * rows * LANES * depth * chans * ways, 6 * 1024 * 1024),
        name="mix",
    )(*weights, *[piece for way in gated for piece in way])


def swap(value, axis, step):
    size = lax.axis_size(axis)
    return lax.ppermute(value, axis, [(i, i ^ step) for i in range(size)])


def exchange(blocks):
    return [b if d == 0 else swap(b, "seq", d) for d, b in enumerate(blocks)]


def on_device(frames_in, w_in, filters, skip_gain, w_out):
    seq, ways = lax.axis_size("seq"), lax.axis_size("ch")
    frames, width = frames_in.shape
    chans = filters.shape[1]
    cpc = chans // (seq * CHUNKS)
    consts = tables(seq * frames // LANES)
    filt = exchange(prepare_filters(filters, seq, cpc))
    weights = [
        w if d == 0 else swap(w, "ch", d) for d, w in enumerate(out_weights(w_out, ways))
    ]
    gate, signal, *sends = project(frames_in, w_in.transpose(1, 0, 2), seq, cpc)
    skip = skip_gain[:, None]
    gated = [[] for _ in range(ways)]
    sig = [exchange([sends[d * CHUNKS + k] for d in range(seq)]) for k in range(CHUNKS)]
    for k in range(CHUNKS):
        y = exchange(convolve(sig[k], filt, consts, k))
        mine = apply_gate(y, gate, signal, skip, k)
        gated[0].append(mine)
        far = swap(mine, "ch", 2)
        gated[2].append(far)
        gated[1].append(swap(mine, "ch", 1))
        gated[3].append(swap(far, "ch", 1))
    return mix(weights, gated)


def solution(mesh):
    in_specs = (P("seq", None), P(None, None, "ch"), P("seq", "ch"), P("ch"), P("ch", None))
    out_specs = P("seq", "ch")
    return jax.shard_map(
        on_device, mesh=mesh, in_specs=in_specs, out_specs=out_specs, check_vma=False
    )
```

```python
import functools
import math

import jax
import jax.numpy as jnp
import numpy as np
from jax import lax
from jax.experimental import pallas as pl
from jax.experimental.pallas import tpu as pltpu
from jax.sharding import PartitionSpec as P

LANES = 128
SMALL = 16
SHARES = (16, 16)
BF16 = jnp.bfloat16
F32 = jnp.float32


def dot(left, right):
    return jnp.dot(left, right, preferred_element_type=F32)


def cost(flops, data):
    return pl.CostEstimate(flops=int(flops), bytes_accessed=int(data), transcendentals=0)


def params(mib):
    return pltpu.CompilerParams(vmem_limit_bytes=mib * 1024 * 1024)


def tables(rows):
    total = rows * LANES
    r = np.arange(rows, dtype=np.float64)
    l = np.arange(LANES, dtype=np.float64)
    first = 2 * np.pi * np.outer(r + 0.25, r) / rows
    twist = 2 * np.pi * np.outer(r + 0.25, l) / total
    second = 2 * np.pi * np.outer(l, l) / LANES
    a_fwd = np.concatenate([np.cos(first), -np.sin(first)], 0)
    a_inv = np.concatenate([np.cos(first).T, -np.sin(first).T], 1) / rows
    c2, s2 = np.cos(second), np.sin(second)
    b_fwd = np.block([[c2, -s2], [s2, c2]])
    b_inv = np.block([[c2, s2], [-s2, c2]]) / LANES
    as_bf = lambda v: jnp.asarray(v.astype(np.float32)).astype(BF16)
    as_f = lambda v: jnp.asarray(v.astype(np.float32))
    return (as_bf(a_fwd), as_bf(b_fwd), as_bf(b_inv), as_bf(a_inv), as_f(np.cos(twist)), as_f(np.sin(twist)))


def seq_peer(step):
    return lax.bitwise_xor(lax.axis_index("seq"), jnp.int32(step))


def block_shapes(seq, cpc, rows):
    return [jax.ShapeDtypeStruct((cpc, rows, LANES), BF16)] * seq


def whole(shape):
    return pl.BlockSpec(tuple(shape), lambda i: (0,) * len(shape))


def tie(value, *after):
    return lax.optimization_barrier((value, *after))[0]


def cut_blocks(turned, outs, cpcs, rows):
    seq = len(outs)
    for d in range(seq):
        peer, start, used = seq_peer(d), 0, 0
        for cpc in cpcs:
            first = pl.multiple_of((start + peer * cpc) * rows, 8)
            part = turned[pl.ds(first, cpc * rows), :]
            outs[d][pl.ds(used, cpc)] = part.reshape(cpc, rows, LANES).astype(BF16)
            start += seq * cpc
            used += cpc


def filter_kernel(seq, cpcs, f_ref, out, turned):
    frames, chans = f_ref.shape
    rows = frames // LANES
    for r in range(rows):
        turned[pl.ds(r, chans, stride=rows), :] = f_ref[pl.ds(r * LANES, LANES), :].astype(F32).T
    start, used = 0, 0
    for cpc in cpcs:
        part = turned[pl.ds(start * rows, seq * cpc * rows), :].reshape(seq, cpc, rows, LANES)
        out[:, pl.ds(used, cpc)] = part.astype(BF16)
        start += seq * cpc
        used += cpc


def prepare_filters(filters, seq, cpcs):
    frames, chans = filters.shape
    rows = frames // LANES
    return pl.pallas_call(
        functools.partial(filter_kernel, seq, cpcs),
        out_shape=jax.ShapeDtypeStruct((seq, chans // seq, rows, LANES), BF16),
        scratch_shapes=[pltpu.VMEM((chans * rows, LANES), F32)],
        compiler_params=params(12),
        cost_estimate=cost(0, 8 * frames * chans),
        name="filter_blocks",
    )(filters)


def project_kernel(seq, cpcs, x_ref, w_ref, _, *refs):
    n = len(cpcs)
    gates, sigs, sends, turned = refs[:n], refs[n : 2 * n], refs[2 * n : -1], refs[-1]
    tile = x_ref.shape[0]
    chans = w_ref.shape[2]
    step = pl.program_id(0)
    rows_here = tile // LANES
    rows = turned.shape[0] // chans
    x = x_ref[...]
    gate = dot(x, w_ref[0]).astype(BF16).astype(F32)
    key = dot(x, w_ref[1]).astype(BF16).astype(F32)
    value = dot(x, w_ref[2]).astype(BF16).astype(F32)
    signal = key * value
    for r in range(rows_here):
        here = slice(r * LANES, (r + 1) * LANES)
        turned_gate, flipped = gate[here].T, signal[here].T
        start = 0
        for k, cpc in enumerate(cpcs):
            span = slice(start, start + seq * cpc)
            gates[k][r] = turned_gate[span].astype(BF16)
            sigs[k][r] = flipped[span].astype(BF16)
            start += seq * cpc
        turned[pl.ds(step * rows_here + r, chans, stride=rows), :] = flipped

    @pl.when(step == pl.num_programs(0) - 1)
    def _():
        cut_blocks(turned, sends, cpcs, rows)


def project(frames_in, w_in, ready, seq, cpcs):
    frames, width = frames_in.shape
    chans = w_in.shape[2]
    rows = frames // LANES
    tile = 512
    send_shapes = block_shapes(seq, sum(cpcs), rows)
    out = pl.pallas_call(
        functools.partial(project_kernel, seq, cpcs),
        grid=(frames // tile,),
        in_specs=[
            pl.BlockSpec((tile, width), lambda i: (i, 0)),
            whole(w_in.shape),
            pl.BlockSpec(memory_space=pl.ANY),
        ],
        out_specs=[
            pl.BlockSpec((tile // LANES, seq * cpc, LANES), lambda i: (i, 0, 0)) for cpc in cpcs
        ]
        * 2
        + [whole(v.shape) for v in send_shapes],
        out_shape=[jax.ShapeDtypeStruct((rows, seq * cpc, LANES), BF16) for cpc in cpcs] * 2
        + send_shapes,
        scratch_shapes=[pltpu.VMEM((chans * rows, LANES), F32)],
        compiler_params=params(58),
        cost_estimate=cost(6 * frames * width * chans, 16 * 1024 * 1024),
        name="project",
    )(frames_in, w_in, ready)
    n = len(cpcs)
    return out[:n], out[n : 2 * n], out[2 * n :]


def gather_rows(grid, blocks, first, cpc):
    rows = blocks[0].shape[1]
    for d, block in enumerate(blocks):
        place = pl.ds(pl.multiple_of(seq_peer(d) * rows, 16), rows)
        grid[:, place, :] = block[pl.ds(first, cpc)]


def twisted(outer, tc, ts):
    full = outer.shape[0] // 2
    parts = []
    for side in (slice(0, LANES), slice(LANES, 2 * LANES)):
        re, im = outer[:full, side], outer[full:, side]
        parts.append(jnp.concatenate([re * tc + im * ts, im * tc - re * ts], 1).astype(BF16))
    return jnp.concatenate(parts, 0)


def forward_pair(grid, c, consts):
    a_fwd, b_fwd, tc, ts = consts
    outer = dot(a_fwd[...], jnp.concatenate([grid[c], grid[c + 1]], 1))
    return dot(twisted(outer, tc, ts), b_fwd[...])


def spectra_kernel(f_ref, a_fwd, b_fwd, tc_ref, ts_ref, out, grid):
    seq, _, rows, _ = f_ref.shape
    chans, full, _ = out.shape
    for j in range(seq):
        grid[:, j * rows : (j + 1) * rows, :] = f_ref[j]
    tc, ts = tc_ref[...], ts_ref[...]
    for c in range(0, chans, 2):
        spec = forward_pair(grid, c, (a_fwd, b_fwd, tc, ts))
        out[c] = spec[:full]
        out[c + 1] = spec[full:]


def filter_spectra(filt, consts):
    a_fwd, b_fwd, _, _, tc, ts = consts
    seq, chans, rows, _ = filt.shape
    full = rows * seq
    return pl.pallas_call(
        spectra_kernel,
        out_shape=jax.ShapeDtypeStruct((chans, full, 2 * LANES), F32),
        scratch_shapes=[pltpu.VMEM((chans, full, LANES), BF16)],
        compiler_params=params(SMALL),
        cost_estimate=cost(chans * full * LANES * LANES * 8, chans * full * LANES * 10),
        name="filter_spectra",
    )(filt, a_fwd, b_fwd, tc, ts)


def conv_kernel(seq, first, skipped, *refs):
    s_refs, rest = refs[:seq], refs[seq:]
    spec_ref, a_fwd, b_fwd, b_inv, a_inv, tc_ref, ts_ref = rest[:7]
    y_refs = rest[7 + skipped : 7 + skipped + seq]
    grid, grid_y, work = rest[7 + skipped + seq :]
    cpc, rows, _ = y_refs[0].shape
    full = rows * seq
    gather_rows(grid, s_refs, first, cpc)
    tc, ts = tc_ref[...], ts_ref[...]
    pairs = [(c, pl.ds(c * full, 2 * full)) for c in range(0, cpc, 2)]
    for c, here in pairs:
        outer = dot(a_fwd[...], jnp.concatenate([grid[c], grid[c + 1]], 1))
        work[here, :] = twisted(outer, tc, ts)
    for c, here in pairs:
        mine = dot(work[here, :], b_fwd[...])
        other = spec_ref[pl.ds(first + c, 2)].reshape(2 * full, 2 * LANES)
        sr, si, fr, fi = mine[:, :LANES], mine[:, LANES:], other[:, :LANES], other[:, LANES:]
        work[here, :] = jnp.concatenate([sr * fr - si * fi, sr * fi + si * fr], 1).astype(BF16)
    for c, here in pairs:
        inner = dot(work[here, :], b_inv[...])
        for i in range(2):
            re, im = inner[i * full : (i + 1) * full, :LANES], inner[i * full : (i + 1) * full, LANES:]
            back = jnp.concatenate([re * tc - im * ts, im * tc + re * ts], 1)
            work[pl.ds((c + i) * full, full), :] = back.astype(BF16)
    for c, here in pairs:
        back = work[here, :]
        re = jnp.concatenate([back[:full, :LANES], back[full:, :LANES]], 1)
        im = jnp.concatenate([back[:full, LANES:], back[full:, LANES:]], 1)
        y = dot(a_inv[...], jnp.concatenate([re, im], 0)).astype(BF16)
        grid_y[c] = y[:, :LANES]
        grid_y[c + 1] = y[:, LANES:]
    for d in range(seq):
        place = pl.ds(pl.multiple_of(seq_peer(d) * rows, 16), rows)
        y_refs[d][...] = grid_y[:, place, :]


def convolve(sig, spec, consts, first, cpc, ready):
    seq = len(sig)
    rows = sig[0].shape[1]
    full = rows * seq
    anywhere = [pl.BlockSpec(memory_space=pl.ANY)] * len(ready)
    ins = (*sig, spec, *consts)
    return pl.pallas_call(
        functools.partial(conv_kernel, seq, first, len(ready)),
        in_specs=[pl.BlockSpec(memory_space=pltpu.VMEM)] * len(ins) + anywhere,
        out_shape=block_shapes(seq, cpc, rows),
        scratch_shapes=[pltpu.VMEM((cpc, full, LANES), BF16)] * 2
        + [pltpu.VMEM((cpc * full, 2 * LANES), BF16)],
        compiler_params=params(SMALL),
        cost_estimate=cost(cpc * full * LANES * LANES * 16, cpc * full * LANES * 12),
        name="convolve",
    )(*ins, *ready)


def gate_kernel(seq, first_chan, *refs):
    gate_ref, sig_ref, skip_ref, out_ref, grid_y = refs[seq:]
    rows, group, _ = out_ref.shape
    part = group // seq * rows
    for d in range(seq):
        start = pl.multiple_of(seq_peer(d) * part, 8)
        grid_y[pl.ds(start, part), :] = refs[d][...].astype(F32).reshape(part, LANES)
    skip = jnp.broadcast_to(skip_ref[...], (LANES, skip_ref.shape[1])).T[
        first_chan : first_chan + group, :1
    ]
    for r in range(rows):
        y = grid_y[pl.ds(r, group, stride=rows), :]
        out_ref[r] = (gate_ref[r].astype(F32) * (y + skip * sig_ref[r].astype(F32))).astype(BF16)


def apply_gate(y, gate, signal, skip, first_chan):
    seq = len(y)
    rows, group, _ = gate.shape
    return pl.pallas_call(
        functools.partial(gate_kernel, seq, first_chan),
        out_shape=jax.ShapeDtypeStruct(gate.shape, BF16),
        scratch_shapes=[pltpu.VMEM((group * rows, LANES), F32)],
        compiler_params=params(SMALL),
        cost_estimate=cost(0, 10 * rows * group * LANES),
        name="apply_gate",
    )(*y, gate, signal, skip)


def out_weights_kernel(ways, w_ref, *outs):
    depth = w_ref.shape[1] // ways
    for d in range(ways):
        peer = lax.bitwise_xor(lax.axis_index("ch"), jnp.int32(d))
        cols = pl.ds(pl.multiple_of(peer * depth, LANES), depth)
        outs[d][...] = w_ref[:, cols].astype(F32).T.astype(BF16)


def out_weights(w_out, ways):
    chans, width = w_out.shape
    return pl.pallas_call(
        functools.partial(out_weights_kernel, ways),
        out_shape=[jax.ShapeDtypeStruct((width // ways, chans), BF16)] * ways,
        compiler_params=params(12),
        cost_estimate=cost(0, 4 * chans * width),
        name="out_weights",
    )(w_out)


def partial_mix(w_refs, g_refs, start, r):
    total = None
    for w_ref, g_ref in zip(w_refs, g_refs):
        rows = slice(start, start + g_ref.shape[1])
        term = dot(w_ref[:, rows], jnp.concatenate([g_ref[r], g_ref[r + 1]], 1))
        total = term if total is None else total + term
    return total


def mix_first_kernel(ways, start, *refs):
    w_refs, g_refs, out_ref = refs[:ways], refs[ways : 2 * ways], refs[-1]
    for r in range(0, g_refs[0].shape[0], 2):
        out_ref[r // 2] = partial_mix(w_refs, g_refs, start, r)


def mix_first(weights, gated, start):
    ways = len(weights)
    rows, group, _ = gated[0].shape
    depth = weights[0].shape[0]
    return pl.pallas_call(
        functools.partial(mix_first_kernel, ways, start),
        out_shape=jax.ShapeDtypeStruct((rows // 2, depth, 2 * LANES), F32),
        compiler_params=params(SMALL),
        cost_estimate=cost(2 * rows * LANES * depth * group * ways, 4 * 1024 * 1024),
        name="mix_first",
    )(*weights, *gated)


def mix_last_kernel(ways, start, *refs):
    w_refs, g_refs = refs[:ways], refs[ways : 2 * ways]
    before, out_ref, held, sems = refs[2 * ways :]
    copies = []
    for r in range(0, g_refs[0].shape[0], 2):
        total = before[r // 2] + partial_mix(w_refs, g_refs, start, r)
        span = pl.ds(r * LANES, 2 * LANES)
        held[span, :] = total.T.astype(BF16)
        copies.append(pltpu.make_async_copy(held.at[span], out_ref.at[span], sems.at[r // 2]))
        copies[-1].start()
    for copy in copies:
        copy.wait()


def mix_last(weights, gated, before, start):
    ways = len(weights)
    rows, group, _ = gated[0].shape
    depth = weights[0].shape[0]
    out = (rows * LANES, depth)
    return pl.pallas_call(
        functools.partial(mix_last_kernel, ways, start),
        out_shape=jax.ShapeDtypeStruct(out, BF16),
        out_specs=pl.BlockSpec(memory_space=pl.ANY),
        scratch_shapes=[pltpu.VMEM(out, BF16), pltpu.SemaphoreType.DMA((rows // 2,))],
        compiler_params=params(SMALL),
        cost_estimate=cost(2 * rows * LANES * depth * group * ways, 6 * 1024 * 1024),
        name="mix_last",
    )(*weights, *gated, before)


def swap(value, axis, step):
    size = lax.axis_size(axis)
    return lax.ppermute(value, axis, [(i, i ^ step) for i in range(size)])


def exchange(blocks):
    return [b if d == 0 else swap(b, "seq", d) for d, b in enumerate(blocks)]


def on_device(frames_in, w_in, filters, skip_gain, w_out):
    seq, ways = lax.axis_size("seq"), lax.axis_size("ch")
    frames, width = frames_in.shape
    chans = filters.shape[1]
    cpcs = [chans * share // (seq * 32) for share in SHARES]
    consts = tables(seq * frames // LANES)
    filt_sends = prepare_filters(filters, seq, cpcs)
    filt = lax.all_to_all(filt_sends, "seq", split_axis=0, concat_axis=0, tiled=True)
    weights = [
        w if d == 0 else swap(w, "ch", d) for d, w in enumerate(out_weights(w_out, ways))
    ]
    gates, sigs, sends = project(frames_in, w_in.transpose(1, 0, 2), filt_sends, seq, cpcs)
    sig = exchange(sends)
    spec = filter_spectra(filt, consts)
    first, start, before, total = 0, 0, [], None
    for k, cpc in enumerate(cpcs):
        y = convolve(sig, spec, consts, first, cpc, [*weights, *before])
        before = [y[0]]
        y = exchange(y)
        mine = apply_gate(y, gates[k], sigs[k], skip_gain[None, :], start)
        far = swap(mine, "ch", 2)
        gated = [mine, swap(mine, "ch", 1), far, swap(far, "ch", 1)]
        if k == 0:
            total = mix_first(weights, gated, start)
        else:
            total = mix_last(weights, gated, total, start)
        first += cpc
        start += seq * cpc
    return total


def solution(mesh):
    in_specs = (P("seq", None), P(None, None, "ch"), P("seq", "ch"), P("ch"), P("ch", None))
    out_specs = P("seq", "ch")
    return jax.shard_map(
        on_device, mesh=mesh, in_specs=in_specs, out_specs=out_specs, check_vma=False
    )
```

```python
import functools
import math

import jax
import jax.numpy as jnp
import numpy as np
from jax import lax
from jax.experimental import pallas as pl
from jax.experimental.pallas import tpu as pltpu
from jax.sharding import PartitionSpec as P

LANES = 128
GROUPS = ((0,1),(4,5,2,3),(6,7))
NEAR = (1, 2, 3)
SMALL = 16
LANES = 128
SMALL = 16
BF16 = jnp.bfloat16
F32 = jnp.float32


def dot(left, right):
    return jnp.dot(left, right, preferred_element_type=F32)


def cost(flops, data):
    return pl.CostEstimate(flops=int(flops), bytes_accessed=int(data), transcendentals=0)


def params(mib):
    return pltpu.CompilerParams(vmem_limit_bytes=mib * 1024 * 1024)


def tables(rows):
    total = rows * LANES
    r = np.arange(rows, dtype=np.float64)
    l = np.arange(LANES, dtype=np.float64)
    first = 2 * np.pi * np.outer(r + 0.25, r) / rows
    twist = 2 * np.pi * np.outer(r + 0.25, l) / total
    second = 2 * np.pi * np.outer(l, l) / LANES
    a_fwd = np.concatenate([np.cos(first), -np.sin(first)], 0)
    a_inv = np.concatenate([np.cos(first).T, -np.sin(first).T], 1) / rows
    c2, s2 = np.cos(second), np.sin(second)
    b_fwd = np.block([[c2, -s2], [s2, c2]])
    b_inv = np.block([[c2, s2], [-s2, c2]]) / LANES
    as_bf = lambda v: jnp.asarray(v.astype(np.float32)).astype(BF16)
    as_f = lambda v: jnp.asarray(v.astype(np.float32))
    return (as_bf(a_fwd), as_bf(b_fwd), as_bf(b_inv), as_bf(a_inv), as_f(np.cos(twist)), as_f(np.sin(twist)))


def seq_peer(step):
    return lax.bitwise_xor(lax.axis_index("seq"), jnp.int32(step))


def block_shapes(seq, cpc, rows):
    return [jax.ShapeDtypeStruct((cpc, rows, LANES), BF16)] * seq


def whole(shape):
    return pl.BlockSpec(tuple(shape), lambda i: (0,) * len(shape))


def tie(value, *after):
    return lax.optimization_barrier((value, *after))[0]


def cut_block(turned, peer, cpd, rows):
    first = pl.multiple_of(peer * (cpd * rows), 8)
    return turned[pl.ds(first, cpd * rows), :].reshape(cpd, rows, LANES).astype(BF16)


def filter_kernel(seq, f_ref, out, turned):
    frames, chans = f_ref.shape
    rows = frames // LANES
    for r in range(rows):
        turned[pl.ds(r, chans, stride=rows), :] = f_ref[pl.ds(r * LANES, LANES), :].astype(F32).T
    for j in range(seq):
        out[j] = cut_block(turned, j, chans // seq, rows)


def prepare_filters(filters, seq):
    frames, chans = filters.shape
    rows = frames // LANES
    return pl.pallas_call(
        functools.partial(filter_kernel, seq),
        out_shape=jax.ShapeDtypeStruct((seq, chans // seq, rows, LANES), BF16),
        scratch_shapes=[pltpu.VMEM((chans * rows, LANES), F32)],
        compiler_params=params(12),
        cost_estimate=cost(0, 8 * frames * chans),
        name="filter_blocks",
    )(filters)


def project_kernel(seq, x_ref, w_ref, _, gates, *refs):
    sends, turned, turned_gate = refs[:seq], refs[seq], refs[seq + 1]
    tile = x_ref.shape[0]
    chans = w_ref.shape[2]
    step = pl.program_id(0)
    rows_here = tile // LANES
    rows = turned.shape[0] // chans
    x = x_ref[...]
    gate = dot(x, w_ref[0]).astype(BF16).astype(F32)
    key = dot(x, w_ref[1]).astype(BF16).astype(F32)
    value = dot(x, w_ref[2]).astype(BF16).astype(F32)
    signal = key * value
    for r in range(rows_here):
        here = slice(r * LANES, (r + 1) * LANES)
        place = pl.ds(step * rows_here + r, chans, stride=rows)
        turned[place, :] = signal[here].T
        turned_gate[place, :] = gate[here].T

    @pl.when(step == pl.num_programs(0) - 1)
    def _():
        for d in range(seq):
            peer = seq_peer(d)
            sends[d][...] = cut_block(turned, peer, chans // seq, rows)
            gates[d] = cut_block(turned_gate, peer, chans // seq, rows)


def project(frames_in, w_in, ready, seq):
    frames, width = frames_in.shape
    chans = w_in.shape[2]
    rows = frames // LANES
    tile = 512
    cpd = chans // seq
    out_shape = [jax.ShapeDtypeStruct((seq, cpd, rows, LANES), BF16)]
    out_shape += block_shapes(seq, cpd, rows)
    gates, *sends = pl.pallas_call(
        functools.partial(project_kernel, seq),
        grid=(frames // tile,),
        in_specs=[
            pl.BlockSpec((tile, width), lambda i: (i, 0)),
            whole(w_in.shape),
            pl.BlockSpec(memory_space=pl.ANY),
        ],
        out_specs=[whole(v.shape) for v in out_shape],
        out_shape=out_shape,
        scratch_shapes=[pltpu.VMEM((chans * rows, LANES), F32)] * 2,
        compiler_params=params(58),
        cost_estimate=cost(6 * frames * width * chans, 16 * 1024 * 1024),
        name="project",
    )(frames_in, w_in, ready)
    return gates, sends


def gather_rows(grid, blocks):
    rows = blocks[0].shape[1]
    for d, block in enumerate(blocks):
        place = pl.ds(pl.multiple_of(seq_peer(d) * rows, 16), rows)
        grid[:, place, :] = block[...]


def twisted(outer, tc, ts):
    full = outer.shape[0] // 2
    parts = []
    for side in (slice(0, LANES), slice(LANES, 2 * LANES)):
        re, im = outer[:full, side], outer[full:, side]
        parts.append(jnp.concatenate([re * tc + im * ts, im * tc - re * ts], 1).astype(BF16))
    return jnp.concatenate(parts, 0)


def forward_pair(grid, c, consts):
    a_fwd, b_fwd, tc, ts = consts
    outer = dot(a_fwd[...], jnp.concatenate([grid[c], grid[c + 1]], 1))
    return dot(twisted(outer, tc, ts), b_fwd[...])


def spectra_kernel(f_ref, a_fwd, b_fwd, tc_ref, ts_ref, out, grid):
    seq, _, rows, _ = f_ref.shape
    chans, full, _ = out.shape
    for j in range(seq):
        grid[:, j * rows : (j + 1) * rows, :] = f_ref[j]
    tc, ts = tc_ref[...], ts_ref[...]
    for c in range(0, chans, 2):
        spec = forward_pair(grid, c, (a_fwd, b_fwd, tc, ts))
        out[c] = spec[:full]
        out[c + 1] = spec[full:]


def filter_spectra(filt, consts):
    a_fwd, b_fwd, _, _, tc, ts = consts
    seq, chans, rows, _ = filt.shape
    full = rows * seq
    return pl.pallas_call(
        spectra_kernel,
        out_shape=jax.ShapeDtypeStruct((chans, full, 2 * LANES), F32),
        scratch_shapes=[pltpu.VMEM((chans, full, LANES), BF16)],
        compiler_params=params(SMALL),
        cost_estimate=cost(chans * full * LANES * LANES * 8, chans * full * LANES * 10),
        name="filter_spectra",
    )(filt, a_fwd, b_fwd, tc, ts)


def conv_kernel(seq, skipped, *refs):
    s_refs, rest = refs[:seq], refs[seq:]
    spec_ref, a_fwd, b_fwd, b_inv, a_inv, tc_ref, ts_ref = rest[:7]
    y_refs = rest[7 + skipped : 7 + skipped + seq]
    grid, grid_y, work = rest[7 + skipped + seq :]
    cpc, rows, _ = y_refs[0].shape
    full = rows * seq
    gather_rows(grid, s_refs)
    tc, ts = tc_ref[...], ts_ref[...]
    pairs = [(c, pl.ds(c * full, 2 * full)) for c in range(0, cpc, 2)]
    for c, here in pairs:
        outer = dot(a_fwd[...], jnp.concatenate([grid[c], grid[c + 1]], 1))
        work[here, :] = twisted(outer, tc, ts)
    for c, here in pairs:
        mine = dot(work[here, :], b_fwd[...])
        other = spec_ref[pl.ds(c, 2)].reshape(2 * full, 2 * LANES)
        sr, si, fr, fi = mine[:, :LANES], mine[:, LANES:], other[:, :LANES], other[:, LANES:]
        work[here, :] = jnp.concatenate([sr * fr - si * fi, sr * fi + si * fr], 1).astype(BF16)
    for c, here in pairs:
        inner = dot(work[here, :], b_inv[...])
        for i in range(2):
            re, im = inner[i * full : (i + 1) * full, :LANES], inner[i * full : (i + 1) * full, LANES:]
            back = jnp.concatenate([re * tc - im * ts, im * tc + re * ts], 1)
            work[pl.ds((c + i) * full, full), :] = back.astype(BF16)
    for c, here in pairs:
        back = work[here, :]
        re = jnp.concatenate([back[:full, :LANES], back[full:, :LANES]], 1)
        im = jnp.concatenate([back[:full, LANES:], back[full:, LANES:]], 1)
        y = dot(a_inv[...], jnp.concatenate([re, im], 0)).astype(BF16)
        grid_y[c] = y[:, :LANES]
        grid_y[c + 1] = y[:, LANES:]
    for d in range(seq):
        place = pl.ds(pl.multiple_of(seq_peer(d) * rows, 16), rows)
        y_refs[d][...] = grid_y[:, place, :]


def convolve(sig, spec, consts, ready):
    seq = len(sig)
    cpc, rows, _ = sig[0].shape
    full = rows * seq
    anywhere = [pl.BlockSpec(memory_space=pl.ANY)] * len(ready)
    ins = (*sig, spec, *consts)
    return pl.pallas_call(
        functools.partial(conv_kernel, seq, len(ready)),
        in_specs=[pl.BlockSpec(memory_space=pltpu.VMEM)] * len(ins) + anywhere,
        out_shape=block_shapes(seq, cpc, rows),
        scratch_shapes=[pltpu.VMEM((cpc, full, LANES), BF16)] * 2
        + [pltpu.VMEM((cpc * full, 2 * LANES), BF16)],
        compiler_params=params(SMALL),
        cost_estimate=cost(cpc * full * LANES * LANES * 16, cpc * full * LANES * 12),
        name="convolve",
    )(*ins, *ready)


def gate_kernel(group, gates, skips, *refs):
    n = len(group)
    y_refs, sig_refs = refs[:n], refs[n : 2 * n]
    out_ref, turned = refs[2 * n :]
    rows, chans, _ = out_ref.shape
    block = chans // n * rows
    for i, d in enumerate(group):
        inner = y_refs[i][...].astype(F32) + skips[d][:, None, :] * sig_refs[i][...].astype(F32)
        value = gates[d].astype(F32) * inner
        turned[pl.ds(i * block, block), :] = value.reshape(block, LANES)
    for r in range(rows):
        out_ref[r] = turned[pl.ds(r, chans, stride=rows), :].astype(BF16)


def apply_gate(group, y, gates, signal, skips):
    cpd, rows, _ = y[0].shape
    chans = len(group) * cpd
    return pl.pallas_call(
        functools.partial(gate_kernel, group),
        out_shape=jax.ShapeDtypeStruct((rows, chans, LANES), BF16),
        scratch_shapes=[pltpu.VMEM((chans * rows, LANES), F32)],
        compiler_params=params(SMALL),
        cost_estimate=cost(0, 10 * rows * chans * LANES),
        name="apply_gate",
    )(gates, skips, *[y[d] for d in group], *[signal[d] for d in group])


def out_weights_kernel(ways, order, w_ref, skip_ref, *refs):
    outs, skips, held, turned = refs[:ways], refs[ways], refs[ways + 1], refs[ways + 2]
    depth = w_ref.shape[1] // ways
    seq, cpd, _ = skips.shape
    held[...] = w_ref[...].astype(F32)
    turned[...] = jnp.broadcast_to(skip_ref[...], (LANES, skip_ref.shape[1])).T
    for d in range(seq):
        skips[d] = turned[pl.ds(pl.multiple_of(seq_peer(d) * cpd, 8), cpd), :]
    for d in range(ways):
        peer = lax.bitwise_xor(lax.axis_index("ch"), jnp.int32(d))
        cols = pl.ds(pl.multiple_of(peer * depth, LANES), depth)
        parts = [
            held[pl.ds(pl.multiple_of(seq_peer(e) * cpd, 8), cpd), cols] for e in order
        ]
        outs[d][...] = jnp.concatenate(parts, 0).T.astype(BF16)


def out_weights(w_out, skip_gain, ways, seq, order):
    chans, width = w_out.shape
    *weights, skips = pl.pallas_call(
        functools.partial(out_weights_kernel, ways, order),
        out_shape=[jax.ShapeDtypeStruct((width // ways, chans), BF16)] * ways
        + [jax.ShapeDtypeStruct((seq, chans // seq, LANES), F32)],
        scratch_shapes=[pltpu.VMEM((chans, width), F32), pltpu.VMEM((chans, LANES), F32)],
        compiler_params=params(SMALL),
        cost_estimate=cost(0, 4 * chans * width),
        name="out_weights",
    )(w_out, skip_gain[None, :])
    return weights, skips


def partial_mix(ways, r):
    total = None
    for w_ref, pieces in ways:
        left = jnp.concatenate([piece[r] for piece in pieces], 0)
        right = jnp.concatenate([piece[r + 1] for piece in pieces], 0)
        term = dot(w_ref[...], jnp.concatenate([left, right], 1))
        total = term if total is None else total + term
    return total


def pair_ways(refs, n):
    return [(refs[i], refs[2 + i * n : 2 + (i + 1) * n]) for i in range(2)]


def mix_early_kernel(n, *refs):
    out_ref = refs[-1]
    for r in range(0, refs[2].shape[0], 2):
        out_ref[r // 2] = partial_mix(pair_ways(refs, n), r)


def mix_early(weights, gated):
    n = len(gated[0])
    rows = gated[0][0].shape[0]
    depth, chans = weights[0].shape
    return pl.pallas_call(
        functools.partial(mix_early_kernel, n),
        out_shape=jax.ShapeDtypeStruct((rows // 2, depth, 2 * LANES), F32),
        compiler_params=params(SMALL),
        cost_estimate=cost(4 * rows * LANES * depth * chans, 4 * 1024 * 1024),
        name="mix_early",
    )(*weights, *gated[0], *gated[1])


def mix_last_kernel(n, *refs):
    before, out_ref, held, sems = refs[2 + 2 * n :]
    copies = []
    for r in range(0, refs[2].shape[0], 2):
        total = before[r // 2] + partial_mix(pair_ways(refs, n), r)
        span = pl.ds(r * LANES, 2 * LANES)
        held[span, :] = total.T.astype(BF16)
        copies.append(pltpu.make_async_copy(held.at[span], out_ref.at[span], sems.at[r // 2]))
        copies[-1].start()
    for copy in copies:
        copy.wait()


def mix_last(weights, gated, before):
    n = len(gated[0])
    rows = gated[0][0].shape[0]
    depth, chans = weights[0].shape
    out = (rows * LANES, depth)
    return pl.pallas_call(
        functools.partial(mix_last_kernel, n),
        out_shape=jax.ShapeDtypeStruct(out, BF16),
        out_specs=pl.BlockSpec(memory_space=pl.ANY),
        scratch_shapes=[pltpu.VMEM(out, BF16), pltpu.SemaphoreType.DMA((rows // 2,))],
        compiler_params=params(SMALL),
        cost_estimate=cost(4 * rows * LANES * depth * chans, 4 * 1024 * 1024),
        name="mix_last",
    )(*weights, *gated[0], *gated[1], before)


def swap(value, axis, step):
    size = lax.axis_size(axis)
    return lax.ppermute(value, axis, [(i, i ^ step) for i in range(size)])


def on_device(frames_in, w_in, filters, skip_gain, w_out):
    seq, ways = lax.axis_size("seq"), lax.axis_size("ch")
    frames, width = frames_in.shape
    chans = filters.shape[1]
    cpd = chans // seq
    consts = tables(seq * frames // LANES)
    filt_sends = prepare_filters(filters, seq)
    filt = lax.all_to_all(filt_sends, "seq", split_axis=0, concat_axis=0, tiled=True)
    unit = max(seq // 8, 1)
    groups = [[d * unit + i for d in g for i in range(unit)] for g in GROUPS]
    order = [d for g in groups for d in g]
    weights, skips = out_weights(w_out, skip_gain, ways, seq, order)
    weights = [w if d == 0 else swap(w, "ch", d) for d, w in enumerate(weights)]
    gates, sends = project(frames_in, w_in.transpose(1, 0, 2), filt_sends, seq)
    sig = [s if d == 0 else swap(s, "seq", d) for d, s in enumerate(sends)]
    y = convolve(sig, filter_spectra(filt, consts), consts, [*weights, skips])
    back = {d: y[0] if d == 0 else swap(y[d], "seq", d) for d in range(seq)}
    mine = [apply_gate(g, back, gates, sends, skips) for g in groups]
    far = [swap(m, "ch", 2) for m in mine]
    near = [swap(m, "ch", 1) for m in mine]
    far = [f if f is far[-1] else tie(f, mine[-1]) for f in far]
    firsts = [swap(f, "ch", 1) for f in far[:-1]]
    total = mix_early(weights[:2], [mine, near])
    last = tie(far[-1], total, *firsts)
    return mix_last(weights[2:], [far[:-1] + [last], firsts + [swap(last, "ch", 1)]], total)


def solution(mesh):
    in_specs = (P("seq", None), P(None, None, "ch"), P("seq", "ch"), P("ch"), P("ch", None))
    out_specs = P("seq", "ch")
    return jax.shard_map(
        on_device, mesh=mesh, in_specs=in_specs, out_specs=out_specs, check_vma=False
    )
```

```python
import functools
import math

import jax
import jax.numpy as jnp
import numpy as np
from jax import lax
from jax.experimental import pallas as pl
from jax.experimental.pallas import tpu as pltpu
from jax.sharding import PartitionSpec as P

LANES = 128
GROUPS = ((4, 5, 0), (2, 3, 1), (6, 7))
NEAR = (1, 2, 3)
SMALL = 16
LANES = 128
SMALL = 16
BF16 = jnp.bfloat16
F32 = jnp.float32


def dot(left, right):
    return jnp.dot(left, right, preferred_element_type=F32)


def cost(flops, data):
    return pl.CostEstimate(flops=int(flops), bytes_accessed=int(data), transcendentals=0)


def params(mib):
    return pltpu.CompilerParams(vmem_limit_bytes=mib * 1024 * 1024)


def tables(rows):
    total = rows * LANES
    r = np.arange(rows, dtype=np.float64)
    l = np.arange(LANES, dtype=np.float64)
    first = 2 * np.pi * np.outer(r + 0.25, r) / rows
    twist = 2 * np.pi * np.outer(r + 0.25, l) / total
    second = 2 * np.pi * np.outer(l, l) / LANES
    a_fwd = np.concatenate([np.cos(first), -np.sin(first)], 0)
    a_inv = np.concatenate([np.cos(first).T, -np.sin(first).T], 1) / rows
    c2, s2 = np.cos(second), np.sin(second)
    b_fwd = np.block([[c2, -s2], [s2, c2]])
    b_inv = np.block([[c2, s2], [-s2, c2]]) / LANES
    as_bf = lambda v: jnp.asarray(v.astype(np.float32)).astype(BF16)
    as_f = lambda v: jnp.asarray(v.astype(np.float32))
    return (as_bf(a_fwd), as_bf(b_fwd), as_bf(b_inv), as_bf(a_inv), as_f(np.cos(twist)), as_f(np.sin(twist)))


def seq_peer(step):
    return lax.bitwise_xor(lax.axis_index("seq"), jnp.int32(step))


def block_shapes(seq, cpc, rows):
    return [jax.ShapeDtypeStruct((cpc, rows, LANES), BF16)] * seq


def whole(shape):
    return pl.BlockSpec(tuple(shape), lambda i: (0,) * len(shape))


def tie(value, *after):
    return lax.optimization_barrier((value, *after))[0]


def cut_block(turned, peer, cpd, rows):
    first = pl.multiple_of(peer * (cpd * rows), 8)
    return turned[pl.ds(first, cpd * rows), :].reshape(cpd, rows, LANES).astype(BF16)


def filter_kernel(seq, f_ref, out, turned):
    frames, chans = f_ref.shape
    rows = frames // LANES
    for r in range(rows):
        turned[pl.ds(r, chans, stride=rows), :] = f_ref[pl.ds(r * LANES, LANES), :].astype(F32).T
    for j in range(seq):
        out[j] = cut_block(turned, j, chans // seq, rows)


def prepare_filters(filters, seq):
    frames, chans = filters.shape
    rows = frames // LANES
    return pl.pallas_call(
        functools.partial(filter_kernel, seq),
        out_shape=jax.ShapeDtypeStruct((seq, chans // seq, rows, LANES), BF16),
        scratch_shapes=[pltpu.VMEM((chans * rows, LANES), F32)],
        compiler_params=params(12),
        cost_estimate=cost(0, 8 * frames * chans),
        name="filter_blocks",
    )(filters)


def project_kernel(seq, x_ref, w_ref, _, gates, *refs):
    sends, turned, turned_gate = refs[:seq], refs[seq], refs[seq + 1]
    tile = x_ref.shape[0]
    chans = w_ref.shape[2]
    step = pl.program_id(0)
    rows_here = tile // LANES
    rows = turned.shape[0] // chans
    x = x_ref[...]
    gate = dot(x, w_ref[0]).astype(BF16).astype(F32)
    key = dot(x, w_ref[1]).astype(BF16).astype(F32)
    value = dot(x, w_ref[2]).astype(BF16).astype(F32)
    signal = key * value
    for r in range(rows_here):
        here = slice(r * LANES, (r + 1) * LANES)
        place = pl.ds(step * rows_here + r, chans, stride=rows)
        turned[place, :] = signal[here].T
        turned_gate[place, :] = gate[here].T

    @pl.when(step == pl.num_programs(0) - 1)
    def _():
        for d in range(seq):
            peer = seq_peer(d)
            sends[d][...] = cut_block(turned, peer, chans // seq, rows)
            gates[d] = cut_block(turned_gate, peer, chans // seq, rows)


def project(frames_in, w_in, ready, seq):
    frames, width = frames_in.shape
    chans = w_in.shape[2]
    rows = frames // LANES
    tile = 512
    cpd = chans // seq
    out_shape = [jax.ShapeDtypeStruct((seq, cpd, rows, LANES), BF16)]
    out_shape += block_shapes(seq, cpd, rows)
    gates, *sends = pl.pallas_call(
        functools.partial(project_kernel, seq),
        grid=(frames // tile,),
        in_specs=[
            pl.BlockSpec((tile, width), lambda i: (i, 0)),
            whole(w_in.shape),
            pl.BlockSpec(memory_space=pl.ANY),
        ],
        out_specs=[whole(v.shape) for v in out_shape],
        out_shape=out_shape,
        scratch_shapes=[pltpu.VMEM((chans * rows, LANES), F32)] * 2,
        compiler_params=params(58),
        cost_estimate=cost(6 * frames * width * chans, 16 * 1024 * 1024),
        name="project",
    )(frames_in, w_in, ready)
    return gates, sends


def gather_rows(grid, blocks):
    rows = blocks[0].shape[1]
    for d, block in enumerate(blocks):
        place = pl.ds(pl.multiple_of(seq_peer(d) * rows, 16), rows)
        grid[:, place, :] = block[...]


def twisted(outer, tc, ts):
    full = outer.shape[0] // 2
    parts = []
    for side in (slice(0, LANES), slice(LANES, 2 * LANES)):
        re, im = outer[:full, side], outer[full:, side]
        parts.append(jnp.concatenate([re * tc + im * ts, im * tc - re * ts], 1).astype(BF16))
    return jnp.concatenate(parts, 0)


def forward_pair(grid, c, consts):
    a_fwd, b_fwd, tc, ts = consts
    outer = dot(a_fwd[...], jnp.concatenate([grid[c], grid[c + 1]], 1))
    return dot(twisted(outer, tc, ts), b_fwd[...])


def spectra_kernel(f_ref, a_fwd, b_fwd, tc_ref, ts_ref, out, grid):
    seq, _, rows, _ = f_ref.shape
    chans, full, _ = out.shape
    for j in range(seq):
        grid[:, j * rows : (j + 1) * rows, :] = f_ref[j]
    tc, ts = tc_ref[...], ts_ref[...]
    for c in range(0, chans, 2):
        spec = forward_pair(grid, c, (a_fwd, b_fwd, tc, ts))
        out[c] = spec[:full]
        out[c + 1] = spec[full:]


def filter_spectra(filt, consts):
    a_fwd, b_fwd, _, _, tc, ts = consts
    seq, chans, rows, _ = filt.shape
    full = rows * seq
    return pl.pallas_call(
        spectra_kernel,
        out_shape=jax.ShapeDtypeStruct((chans, full, 2 * LANES), F32),
        scratch_shapes=[pltpu.VMEM((chans, full, LANES), BF16)],
        compiler_params=params(SMALL),
        cost_estimate=cost(chans * full * LANES * LANES * 8, chans * full * LANES * 10),
        name="filter_spectra",
    )(filt, a_fwd, b_fwd, tc, ts)


def conv_kernel(seq, skipped, *refs):
    s_refs, rest = refs[:seq], refs[seq:]
    spec_ref, a_fwd, b_fwd, b_inv, a_inv, tc_ref, ts_ref = rest[:7]
    y_refs = rest[7 + skipped : 7 + skipped + seq]
    grid, grid_y, work = rest[7 + skipped + seq :]
    cpc, rows, _ = y_refs[0].shape
    full = rows * seq
    gather_rows(grid, s_refs)
    tc, ts = tc_ref[...], ts_ref[...]
    pairs = [(c, pl.ds(c * full, 2 * full)) for c in range(0, cpc, 2)]
    for c, here in pairs:
        outer = dot(a_fwd[...], jnp.concatenate([grid[c], grid[c + 1]], 1))
        work[here, :] = twisted(outer, tc, ts)
    for c, here in pairs:
        mine = dot(work[here, :], b_fwd[...])
        other = spec_ref[pl.ds(c, 2)].reshape(2 * full, 2 * LANES)
        sr, si, fr, fi = mine[:, :LANES], mine[:, LANES:], other[:, :LANES], other[:, LANES:]
        work[here, :] = jnp.concatenate([sr * fr - si * fi, sr * fi + si * fr], 1).astype(BF16)
    for c, here in pairs:
        inner = dot(work[here, :], b_inv[...])
        for i in range(2):
            re, im = inner[i * full : (i + 1) * full, :LANES], inner[i * full : (i + 1) * full, LANES:]
            back = jnp.concatenate([re * tc - im * ts, im * tc + re * ts], 1)
            work[pl.ds((c + i) * full, full), :] = back.astype(BF16)
    for c, here in pairs:
        back = work[here, :]
        re = jnp.concatenate([back[:full, :LANES], back[full:, :LANES]], 1)
        im = jnp.concatenate([back[:full, LANES:], back[full:, LANES:]], 1)
        y = dot(a_inv[...], jnp.concatenate([re, im], 0)).astype(BF16)
        grid_y[c] = y[:, :LANES]
        grid_y[c + 1] = y[:, LANES:]
    for d in range(seq):
        place = pl.ds(pl.multiple_of(seq_peer(d) * rows, 16), rows)
        y_refs[d][...] = grid_y[:, place, :]


def convolve(sig, spec, consts, ready):
    seq = len(sig)
    cpc, rows, _ = sig[0].shape
    full = rows * seq
    anywhere = [pl.BlockSpec(memory_space=pl.ANY)] * len(ready)
    ins = (*sig, spec, *consts)
    return pl.pallas_call(
        functools.partial(conv_kernel, seq, len(ready)),
        in_specs=[pl.BlockSpec(memory_space=pltpu.VMEM)] * len(ins) + anywhere,
        out_shape=block_shapes(seq, cpc, rows),
        scratch_shapes=[pltpu.VMEM((cpc, full, LANES), BF16)] * 2
        + [pltpu.VMEM((cpc * full, 2 * LANES), BF16)],
        compiler_params=params(SMALL),
        cost_estimate=cost(cpc * full * LANES * LANES * 16, cpc * full * LANES * 12),
        name="convolve",
    )(*ins, *ready)


def gate_kernel(group, gates, skips, *refs):
    n = len(group)
    y_refs, sig_refs = refs[:n], refs[n : 2 * n]
    out_ref, turned = refs[2 * n :]
    rows, chans, _ = out_ref.shape
    block = chans // n * rows
    for i, d in enumerate(group):
        inner = y_refs[i][...].astype(F32) + skips[d][:, None, :] * sig_refs[i][...].astype(F32)
        value = gates[d].astype(F32) * inner
        turned[pl.ds(i * block, block), :] = value.reshape(block, LANES)
    for r in range(rows):
        out_ref[r] = turned[pl.ds(r, chans, stride=rows), :].astype(BF16)


def apply_gate(group, y, gates, signal, skips):
    cpd, rows, _ = y[0].shape
    chans = len(group) * cpd
    return pl.pallas_call(
        functools.partial(gate_kernel, group),
        out_shape=jax.ShapeDtypeStruct((rows, chans, LANES), BF16),
        scratch_shapes=[pltpu.VMEM((chans * rows, LANES), F32)],
        compiler_params=params(SMALL),
        cost_estimate=cost(0, 10 * rows * chans * LANES),
        name="apply_gate",
    )(gates, skips, *[y[d] for d in group], *[signal[d] for d in group])


def out_weights_kernel(ways, order, w_ref, skip_ref, *refs):
    outs, skips, held, turned = refs[:ways], refs[ways], refs[ways + 1], refs[ways + 2]
    depth = w_ref.shape[1] // ways
    seq, cpd, _ = skips.shape
    held[...] = w_ref[...].astype(F32)
    turned[...] = jnp.broadcast_to(skip_ref[...], (LANES, skip_ref.shape[1])).T
    for d in range(seq):
        skips[d] = turned[pl.ds(pl.multiple_of(seq_peer(d) * cpd, 8), cpd), :]
    for d in range(ways):
        peer = lax.bitwise_xor(lax.axis_index("ch"), jnp.int32(d))
        cols = pl.ds(pl.multiple_of(peer * depth, LANES), depth)
        parts = [
            held[pl.ds(pl.multiple_of(seq_peer(e) * cpd, 8), cpd), cols] for e in order
        ]
        outs[d][...] = jnp.concatenate(parts, 0).T.astype(BF16)


def out_weights(w_out, skip_gain, ways, seq, order):
    chans, width = w_out.shape
    *weights, skips = pl.pallas_call(
        functools.partial(out_weights_kernel, ways, order),
        out_shape=[jax.ShapeDtypeStruct((width // ways, chans), BF16)] * ways
        + [jax.ShapeDtypeStruct((seq, chans // seq, LANES), F32)],
        scratch_shapes=[pltpu.VMEM((chans, width), F32), pltpu.VMEM((chans, LANES), F32)],
        compiler_params=params(SMALL),
        cost_estimate=cost(0, 4 * chans * width),
        name="out_weights",
    )(w_out, skip_gain[None, :])
    return weights, skips


def partial_mix(ways, r):
    total = None
    for w_ref, pieces in ways:
        left = jnp.concatenate([piece[r] for piece in pieces], 0)
        right = jnp.concatenate([piece[r + 1] for piece in pieces], 0)
        term = dot(w_ref[...], jnp.concatenate([left, right], 1))
        total = term if total is None else total + term
    return total


def pair_ways(refs, n):
    return [(refs[i], refs[2 + i * n : 2 + (i + 1) * n]) for i in range(2)]


def mix_early_kernel(n, *refs):
    out_ref = refs[-1]
    for r in range(0, refs[2].shape[0], 2):
        out_ref[r // 2] = partial_mix(pair_ways(refs, n), r)


def mix_early(weights, gated):
    n = len(gated[0])
    rows = gated[0][0].shape[0]
    depth, chans = weights[0].shape
    return pl.pallas_call(
        functools.partial(mix_early_kernel, n),
        out_shape=jax.ShapeDtypeStruct((rows // 2, depth, 2 * LANES), F32),
        compiler_params=params(SMALL),
        cost_estimate=cost(4 * rows * LANES * depth * chans, 4 * 1024 * 1024),
        name="mix_early",
    )(*weights, *gated[0], *gated[1])


def mix_last_kernel(n, *refs):
    before, out_ref, held, sems = refs[2 + 2 * n :]
    copies = []
    for r in range(0, refs[2].shape[0], 2):
        total = before[r // 2] + partial_mix(pair_ways(refs, n), r)
        span = pl.ds(r * LANES, 2 * LANES)
        held[span, :] = total.T.astype(BF16)
        copies.append(pltpu.make_async_copy(held.at[span], out_ref.at[span], sems.at[r // 2]))
        copies[-1].start()
    for copy in copies:
        copy.wait()


def mix_last(weights, gated, before):
    n = len(gated[0])
    rows = gated[0][0].shape[0]
    depth, chans = weights[0].shape
    out = (rows * LANES, depth)
    return pl.pallas_call(
        functools.partial(mix_last_kernel, n),
        out_shape=jax.ShapeDtypeStruct(out, BF16),
        out_specs=pl.BlockSpec(memory_space=pl.ANY),
        scratch_shapes=[pltpu.VMEM(out, BF16), pltpu.SemaphoreType.DMA((rows // 2,))],
        compiler_params=params(SMALL),
        cost_estimate=cost(4 * rows * LANES * depth * chans, 4 * 1024 * 1024),
        name="mix_last",
    )(*weights, *gated[0], *gated[1], before)


def swap(value, axis, step):
    size = lax.axis_size(axis)
    return lax.ppermute(value, axis, [(i, i ^ step) for i in range(size)])


def on_device(frames_in, w_in, filters, skip_gain, w_out):
    seq, ways = lax.axis_size("seq"), lax.axis_size("ch")
    frames, width = frames_in.shape
    chans = filters.shape[1]
    cpd = chans // seq
    consts = tables(seq * frames // LANES)
    filt_sends = prepare_filters(filters, seq)
    filt = lax.all_to_all(filt_sends, "seq", split_axis=0, concat_axis=0, tiled=True)
    unit = max(seq // 8, 1)
    groups = [[d * unit + i for d in g for i in range(unit)] for g in GROUPS]
    order = [d for g in groups for d in g]
    weights, skips = out_weights(w_out, skip_gain, ways, seq, order)
    weights = [w if d == 0 else swap(w, "ch", d) for d, w in enumerate(weights)]
    gates, sends = project(frames_in, w_in.transpose(1, 0, 2), filt_sends, seq)
    sig = [s if d == 0 else swap(s, "seq", d) for d, s in enumerate(sends)]
    y = convolve(sig, filter_spectra(filt, consts), consts, [*weights, skips])
    back = {d: y[0] if d == 0 else swap(y[d], "seq", d) for d in range(seq)}
    mine = [apply_gate(g, back, gates, sends, skips) for g in groups]
    far = [swap(m, "ch", 2) for m in mine]
    near = [swap(m, "ch", 1) for m in mine]
    far = [f if f is far[-1] else tie(f, mine[-1]) for f in far]
    firsts = [swap(f, "ch", 1) for f in far[:-1]]
    total = mix_early(weights[:2], [mine, near])
    last = tie(far[-1], total, *firsts)
    return mix_last(weights[2:], [far[:-1] + [last], firsts + [swap(last, "ch", 1)]], total)


def solution(mesh):
    in_specs = (P("seq", None), P(None, None, "ch"), P("seq", "ch"), P("ch"), P("ch", None))
    out_specs = P("seq", "ch")
    return jax.shard_map(
        on_device, mesh=mesh, in_specs=in_specs, out_specs=out_specs, check_vma=False
    )
```

```python
import functools
import math

import jax
import jax.numpy as jnp
import numpy as np
from jax import lax
from jax.experimental import pallas as pl
from jax.experimental.pallas import tpu as pltpu
from jax.sharding import PartitionSpec as P

LANES = 128
GROUPS = ((4, 5, 0), (2, 3, 1), (6, 7))
NEAR = (1, 2, 3)
SMALL = 16
LANES = 128
SMALL = 16
BF16 = jnp.bfloat16
F32 = jnp.float32


def dot(left, right):
    return jnp.dot(left, right, preferred_element_type=F32)


def cost(flops, data):
    return pl.CostEstimate(flops=int(flops), bytes_accessed=int(data), transcendentals=0)


def params(mib):
    return pltpu.CompilerParams(vmem_limit_bytes=mib * 1024 * 1024)


def tables(rows):
    total = rows * LANES
    r = np.arange(rows, dtype=np.float64)
    l = np.arange(LANES, dtype=np.float64)
    first = 2 * np.pi * np.outer(r + 0.25, r) / rows
    twist = 2 * np.pi * np.outer(r + 0.25, l) / total
    second = 2 * np.pi * np.outer(l, l) / LANES
    a_fwd = np.concatenate([np.cos(first), -np.sin(first)], 0)
    a_inv = np.concatenate([np.cos(first).T, -np.sin(first).T], 1) / rows
    c2, s2 = np.cos(second), np.sin(second)
    b_fwd = np.block([[c2, -s2], [s2, c2]])
    b_inv = np.block([[c2, s2], [-s2, c2]]) / LANES
    as_bf = lambda v: jnp.asarray(v.astype(np.float32)).astype(BF16)
    as_f = lambda v: jnp.asarray(v.astype(np.float32))
    return (as_bf(a_fwd), as_bf(b_fwd), as_bf(b_inv), as_bf(a_inv), as_f(np.cos(twist)), as_f(np.sin(twist)))


def seq_peer(step):
    return lax.bitwise_xor(lax.axis_index("seq"), jnp.int32(step))


def block_shapes(seq, cpc, rows):
    return [jax.ShapeDtypeStruct((cpc, rows, LANES), BF16)] * seq


def strided_scratch(chans, rows):
    return pltpu.VMEM((chans * rows + rows, LANES), F32)


def whole(shape):
    return pl.BlockSpec(tuple(shape), lambda i: (0,) * len(shape))


def tie(value, *after):
    return lax.optimization_barrier((value, *after))[0]


def cut_block(turned, peer, cpd, rows):
    first = pl.multiple_of(peer * (cpd * rows), 8)
    return turned[pl.ds(first, cpd * rows), :].reshape(cpd, rows, LANES).astype(BF16)


def filter_kernel(seq, f_ref, out, turned):
    frames, chans = f_ref.shape
    rows = frames // LANES
    for r in range(rows):
        turned[pl.ds(r, chans, stride=rows), :] = f_ref[pl.ds(r * LANES, LANES), :].astype(F32).T
    for j in range(seq):
        out[j] = cut_block(turned, j, chans // seq, rows)


def prepare_filters(filters, seq):
    frames, chans = filters.shape
    rows = frames // LANES
    return pl.pallas_call(
        functools.partial(filter_kernel, seq),
        out_shape=jax.ShapeDtypeStruct((seq, chans // seq, rows, LANES), BF16),
        scratch_shapes=[strided_scratch(chans, rows)],
        compiler_params=params(12),
        cost_estimate=cost(0, 8 * frames * chans),
        name="filter_blocks",
    )(filters)


def project_kernel(seq, x_ref, w_ref, _, gates, *refs):
    sends, turned, turned_gate = refs[:seq], refs[seq], refs[seq + 1]
    tile = x_ref.shape[0]
    chans = w_ref.shape[2]
    step = pl.program_id(0)
    rows_here = tile // LANES
    rows = turned.shape[0] // chans
    x = x_ref[...]
    gate = dot(x, w_ref[0]).astype(BF16).astype(F32)
    key = dot(x, w_ref[1]).astype(BF16).astype(F32)
    value = dot(x, w_ref[2]).astype(BF16).astype(F32)
    signal = key * value
    for r in range(rows_here):
        here = slice(r * LANES, (r + 1) * LANES)
        place = pl.ds(step * rows_here + r, chans, stride=rows)
        turned[place, :] = signal[here].T
        turned_gate[place, :] = gate[here].T

    @pl.when(step == pl.num_programs(0) - 1)
    def _():
        for d in range(seq):
            peer = seq_peer(d)
            sends[d][...] = cut_block(turned, peer, chans // seq, rows)
            gates[d] = cut_block(turned_gate, peer, chans // seq, rows)


def project(frames_in, w_in, ready, seq):
    frames, width = frames_in.shape
    chans = w_in.shape[2]
    rows = frames // LANES
    tile = 512
    cpd = chans // seq
    out_shape = [jax.ShapeDtypeStruct((seq, cpd, rows, LANES), BF16)]
    out_shape += block_shapes(seq, cpd, rows)
    gates, *sends = pl.pallas_call(
        functools.partial(project_kernel, seq),
        grid=(frames // tile,),
        in_specs=[
            pl.BlockSpec((tile, width), lambda i: (i, 0)),
            whole(w_in.shape),
            pl.BlockSpec(memory_space=pl.ANY),
        ],
        out_specs=[whole(v.shape) for v in out_shape],
        out_shape=out_shape,
        scratch_shapes=[strided_scratch(chans, rows)] * 2,
        compiler_params=params(58),
        cost_estimate=cost(6 * frames * width * chans, 16 * 1024 * 1024),
        name="project",
    )(frames_in, w_in, ready)
    return gates, sends


def gather_rows(grid, blocks):
    rows = blocks[0].shape[1]
    for d, block in enumerate(blocks):
        place = pl.ds(pl.multiple_of(seq_peer(d) * rows, 16), rows)
        grid[:, place, :] = block[...]


def twisted(outer, tc, ts):
    full = outer.shape[0] // 2
    parts = []
    for side in (slice(0, LANES), slice(LANES, 2 * LANES)):
        re, im = outer[:full, side], outer[full:, side]
        parts.append(jnp.concatenate([re * tc + im * ts, im * tc - re * ts], 1).astype(BF16))
    return jnp.concatenate(parts, 0)


def forward_pair(grid, c, consts):
    a_fwd, b_fwd, tc, ts = consts
    outer = dot(a_fwd[...], jnp.concatenate([grid[c], grid[c + 1]], 1))
    return dot(twisted(outer, tc, ts), b_fwd[...])


def spectra_kernel(f_ref, a_fwd, b_fwd, tc_ref, ts_ref, out, grid):
    seq, _, rows, _ = f_ref.shape
    chans, full, _ = out.shape
    for j in range(seq):
        grid[:, j * rows : (j + 1) * rows, :] = f_ref[j]
    tc, ts = tc_ref[...], ts_ref[...]
    for c in range(0, chans, 2):
        spec = forward_pair(grid, c, (a_fwd, b_fwd, tc, ts))
        out[c] = spec[:full]
        out[c + 1] = spec[full:]


def filter_spectra(filt, consts):
    a_fwd, b_fwd, _, _, tc, ts = consts
    seq, chans, rows, _ = filt.shape
    full = rows * seq
    return pl.pallas_call(
        spectra_kernel,
        out_shape=jax.ShapeDtypeStruct((chans, full, 2 * LANES), F32),
        scratch_shapes=[pltpu.VMEM((chans, full, LANES), BF16)],
        compiler_params=params(SMALL),
        cost_estimate=cost(chans * full * LANES * LANES * 8, chans * full * LANES * 10),
        name="filter_spectra",
    )(filt, a_fwd, b_fwd, tc, ts)


def conv_kernel(seq, skipped, *refs):
    s_refs, rest = refs[:seq], refs[seq:]
    spec_ref, a_fwd, b_fwd, b_inv, a_inv, tc_ref, ts_ref = rest[:7]
    y_refs = rest[7 + skipped : 7 + skipped + seq]
    grid, grid_y, work = rest[7 + skipped + seq :]
    cpc, rows, _ = y_refs[0].shape
    full = rows * seq
    gather_rows(grid, s_refs)
    tc, ts = tc_ref[...], ts_ref[...]
    pairs = [(c, pl.ds(c * full, 2 * full)) for c in range(0, cpc, 2)]
    for c, here in pairs:
        outer = dot(a_fwd[...], jnp.concatenate([grid[c], grid[c + 1]], 1))
        work[here, :] = twisted(outer, tc, ts)
    for c, here in pairs:
        mine = dot(work[here, :], b_fwd[...])
        other = spec_ref[pl.ds(c, 2)].reshape(2 * full, 2 * LANES)
        sr, si, fr, fi = mine[:, :LANES], mine[:, LANES:], other[:, :LANES], other[:, LANES:]
        work[here, :] = jnp.concatenate([sr * fr - si * fi, sr * fi + si * fr], 1).astype(BF16)
    for c, here in pairs:
        inner = dot(work[here, :], b_inv[...])
        for i in range(2):
            re, im = inner[i * full : (i + 1) * full, :LANES], inner[i * full : (i + 1) * full, LANES:]
            back = jnp.concatenate([re * tc - im * ts, im * tc + re * ts], 1)
            work[pl.ds((c + i) * full, full), :] = back.astype(BF16)
    for c, here in pairs:
        back = work[here, :]
        re = jnp.concatenate([back[:full, :LANES], back[full:, :LANES]], 1)
        im = jnp.concatenate([back[:full, LANES:], back[full:, LANES:]], 1)
        y = dot(a_inv[...], jnp.concatenate([re, im], 0)).astype(BF16)
        grid_y[c] = y[:, :LANES]
        grid_y[c + 1] = y[:, LANES:]
    for d in range(seq):
        place = pl.ds(pl.multiple_of(seq_peer(d) * rows, 16), rows)
        y_refs[d][...] = grid_y[:, place, :]


def convolve(sig, spec, consts, ready):
    seq = len(sig)
    cpc, rows, _ = sig[0].shape
    full = rows * seq
    anywhere = [pl.BlockSpec(memory_space=pl.ANY)] * len(ready)
    ins = (*sig, spec, *consts)
    return pl.pallas_call(
        functools.partial(conv_kernel, seq, len(ready)),
        in_specs=[pl.BlockSpec(memory_space=pltpu.VMEM)] * len(ins) + anywhere,
        out_shape=block_shapes(seq, cpc, rows),
        scratch_shapes=[pltpu.VMEM((cpc, full, LANES), BF16)] * 2
        + [pltpu.VMEM((cpc * full, 2 * LANES), BF16)],
        compiler_params=params(SMALL),
        cost_estimate=cost(cpc * full * LANES * LANES * 16, cpc * full * LANES * 12),
        name="convolve",
    )(*ins, *ready)


def gate_kernel(group, gates, skips, *refs):
    n = len(group)
    y_refs, sig_refs = refs[:n], refs[n : 2 * n]
    out_ref, turned = refs[2 * n :]
    rows, chans, _ = out_ref.shape
    block = chans // n * rows
    for i, d in enumerate(group):
        inner = y_refs[i][...].astype(F32) + skips[d][:, None, :] * sig_refs[i][...].astype(F32)
        value = gates[d].astype(F32) * inner
        turned[pl.ds(i * block, block), :] = value.reshape(block, LANES)
    for r in range(rows):
        out_ref[r] = turned[pl.ds(r, chans, stride=rows), :].astype(BF16)


def apply_gate(group, y, gates, signal, skips):
    cpd, rows, _ = y[0].shape
    chans = len(group) * cpd
    return pl.pallas_call(
        functools.partial(gate_kernel, group),
        out_shape=jax.ShapeDtypeStruct((rows, chans, LANES), BF16),
        scratch_shapes=[strided_scratch(chans, rows)],
        compiler_params=params(SMALL),
        cost_estimate=cost(0, 10 * rows * chans * LANES),
        name="apply_gate",
    )(gates, skips, *[y[d] for d in group], *[signal[d] for d in group])


def out_weights_kernel(ways, order, w_ref, skip_ref, *refs):
    outs, skips, held, turned = refs[:ways], refs[ways], refs[ways + 1], refs[ways + 2]
    depth = w_ref.shape[1] // ways
    seq, cpd, _ = skips.shape
    held[...] = w_ref[...].astype(F32)
    turned[...] = jnp.broadcast_to(skip_ref[...], (LANES, skip_ref.shape[1])).T
    for d in range(seq):
        skips[d] = turned[pl.ds(pl.multiple_of(seq_peer(d) * cpd, 8), cpd), :]
    for d in range(ways):
        peer = lax.bitwise_xor(lax.axis_index("ch"), jnp.int32(d))
        cols = pl.ds(pl.multiple_of(peer * depth, LANES), depth)
        parts = [
            held[pl.ds(pl.multiple_of(seq_peer(e) * cpd, 8), cpd), cols] for e in order
        ]
        outs[d][...] = jnp.concatenate(parts, 0).T.astype(BF16)


def out_weights(w_out, skip_gain, ways, seq, order):
    chans, width = w_out.shape
    *weights, skips = pl.pallas_call(
        functools.partial(out_weights_kernel, ways, order),
        out_shape=[jax.ShapeDtypeStruct((width // ways, chans), BF16)] * ways
        + [jax.ShapeDtypeStruct((seq, chans // seq, LANES), F32)],
        scratch_shapes=[pltpu.VMEM((chans, width), F32), pltpu.VMEM((chans, LANES), F32)],
        compiler_params=params(SMALL),
        cost_estimate=cost(0, 4 * chans * width),
        name="out_weights",
    )(w_out, skip_gain[None, :])
    return weights, skips


def partial_mix(ways, r):
    total = None
    for w_ref, pieces in ways:
        left = jnp.concatenate([piece[r] for piece in pieces], 0)
        right = jnp.concatenate([piece[r + 1] for piece in pieces], 0)
        term = dot(w_ref[...], jnp.concatenate([left, right], 1))
        total = term if total is None else total + term
    return total


def pair_ways(refs, n):
    return [(refs[i], refs[2 + i * n : 2 + (i + 1) * n]) for i in range(2)]


def mix_early_kernel(n, *refs):
    out_ref = refs[-1]
    for r in range(0, refs[2].shape[0], 2):
        out_ref[r // 2] = partial_mix(pair_ways(refs, n), r)


def mix_early(weights, gated):
    n = len(gated[0])
    rows = gated[0][0].shape[0]
    depth, chans = weights[0].shape
    return pl.pallas_call(
        functools.partial(mix_early_kernel, n),
        out_shape=jax.ShapeDtypeStruct((rows // 2, depth, 2 * LANES), F32),
        compiler_params=params(SMALL),
        cost_estimate=cost(4 * rows * LANES * depth * chans, 4 * 1024 * 1024),
        name="mix_early",
    )(*weights, *gated[0], *gated[1])


def mix_last_kernel(n, *refs):
    before, out_ref, held, sems = refs[2 + 2 * n :]
    copies = []
    for r in range(0, refs[2].shape[0], 2):
        total = before[r // 2] + partial_mix(pair_ways(refs, n), r)
        span = pl.ds(r * LANES, 2 * LANES)
        held[span, :] = total.T.astype(BF16)
        copies.append(pltpu.make_async_copy(held.at[span], out_ref.at[span], sems.at[r // 2]))
        copies[-1].start()
    for copy in copies:
        copy.wait()


def mix_last(weights, gated, before):
    n = len(gated[0])
    rows = gated[0][0].shape[0]
    depth, chans = weights[0].shape
    out = (rows * LANES, depth)
    return pl.pallas_call(
        functools.partial(mix_last_kernel, n),
        out_shape=jax.ShapeDtypeStruct(out, BF16),
        out_specs=pl.BlockSpec(memory_space=pl.ANY),
        scratch_shapes=[pltpu.VMEM(out, BF16), pltpu.SemaphoreType.DMA((rows // 2,))],
        compiler_params=params(SMALL),
        cost_estimate=cost(4 * rows * LANES * depth * chans, 4 * 1024 * 1024),
        name="mix_last",
    )(*weights, *gated[0], *gated[1], before)


def swap(value, axis, step):
    size = lax.axis_size(axis)
    return lax.ppermute(value, axis, [(i, i ^ step) for i in range(size)])


def on_device(frames_in, w_in, filters, skip_gain, w_out):
    seq, ways = lax.axis_size("seq"), lax.axis_size("ch")
    frames, width = frames_in.shape
    chans = filters.shape[1]
    cpd = chans // seq
    consts = tables(seq * frames // LANES)
    filt_sends = prepare_filters(filters, seq)
    filt = lax.all_to_all(filt_sends, "seq", split_axis=0, concat_axis=0, tiled=True)
    unit = max(seq // 8, 1)
    groups = [[d * unit + i for d in g for i in range(unit)] for g in GROUPS]
    order = [d for g in groups for d in g]
    weights, skips = out_weights(w_out, skip_gain, ways, seq, order)
    weights = [w if d == 0 else swap(w, "ch", d) for d, w in enumerate(weights)]
    gates, sends = project(frames_in, w_in.transpose(1, 0, 2), filt_sends, seq)
    sig = [s if d == 0 else swap(s, "seq", d) for d, s in enumerate(sends)]
    y = convolve(sig, filter_spectra(filt, consts), consts, [*weights, skips])
    back = {d: y[0] if d == 0 else swap(y[d], "seq", d) for d in range(seq)}
    mine = [apply_gate(g, back, gates, sends, skips) for g in groups]
    far = [swap(m, "ch", 2) for m in mine]
    near = [swap(m, "ch", 1) for m in mine]
    far = [f if f is far[-1] else tie(f, mine[-1]) for f in far]
    firsts = [swap(f, "ch", 1) for f in far[:-1]]
    total = mix_early(weights[:2], [mine, near])
    last = tie(far[-1], total, *firsts)
    return mix_last(weights[2:], [far[:-1] + [last], firsts + [swap(last, "ch", 1)]], total)


def solution(mesh):
    in_specs = (P("seq", None), P(None, None, "ch"), P("seq", "ch"), P("ch"), P("ch", None))
    out_specs = P("seq", "ch")
    return jax.shard_map(
        on_device, mesh=mesh, in_specs=in_specs, out_specs=out_specs, check_vma=False
    )
```
